512 devices in a mesh: row: 32 (over x, z), col: 16 (over y, core).
Axes of the slice: x: 4, y: 8, z: 8, core: 2. Of those that a mesh axis runs over, the one named last changes fastest.
Arguments:
- row_embeds: bfloat16 [32768, 1024], P('row', 'col'), may hold values from -4 to 4
- panel_embeds: bfloat16 [512, 1024], P(None, 'col'), may hold values from -4 to 4
- trailing: float32 [32768, 8192], P('row', 'col'), may hold values from -6 to 6
Outputs:
- panel: float32 [32768, 512], P('row', 'col')
- updated: float32 [32768, 8192], P('row', 'col')
The draws below stay inside these ranges and needn't reach their ends.
All inputs are finite; a program needn't handle non-finite values.
Results may differ from the reference program's by a relative error of at most 0.0003.
Values may be sent and summed in bfloat16 or wider, within the bound.
A program may use at most 64 MiB of HBM per device.

```python
import jax
import jax.numpy as jnp
from jax import lax

EMBED = 1024
PANEL = 512
ROWS = 32768
SLAB = 8192


SPREAD = 2.0


def centre_values(key):
    centre_key = jax.random.fold_in(key, 21)
    centres = jax.random.truncated_normal(centre_key, -4.0, 4.0, (PANEL, EMBED), jnp.float32)
    return centres


def draw_row_embeds(key, part):
    centres = centre_values(key)
    key = jax.random.fold_in(key, 3)
    scale = (SPREAD / EMBED) ** 0.5
    owners = jax.random.randint(jax.random.fold_in(key, 7), (ROWS,), 0, PANEL)
    likeness = jax.random.uniform(jax.random.fold_in(key, 8), (ROWS, 1), jnp.float32, 0.5, 0.9)
    noise = jax.random.truncated_normal(key, -4.0, 4.0, (ROWS, EMBED), jnp.float32)
    values = likeness * centres[owners] + jnp.sqrt(1.0 - likeness * likeness) * noise
    return (values * scale).astype(jnp.bfloat16)


def draw_panel_embeds(key, part):
    centres = centre_values(key)
    scale = (SPREAD / EMBED) ** 0.5
    values = centres
    return (values * scale).astype(jnp.bfloat16)


def block_scale(stream_key, shape, shards, low, top_value):
    loudness = 1.0
    for axis_at, shards_of in shards:
        steps = jax.random.uniform(jax.random.fold_in(jax.random.fold_in(stream_key, 6), axis_at), (shards_of,), jnp.float32, low / len(shards), top_value / len(shards))
        loudness = loudness * jnp.repeat(jnp.exp(steps), shape[axis_at] // shards_of).reshape((-1,) + (1,) * (len(shape) - 1 - axis_at))
    return loudness


def bell_draw(rng, extent, deviation, reach, shards=(), kind=jnp.bfloat16):
    result = jax.random.normal(rng, extent, jnp.float32) * deviation
    if len(shards) > 0:
        result = block_scale(rng, extent, shards, -0.22, 0.18) * result
    return jnp.clip(result, min=-reach, max=reach).astype(kind)


def setup_inputs(seed: int = 0) -> dict:
    splits = jax.random.split(jax.random.key(seed), 4)
    return {
        "row_embeds": draw_row_embeds(jax.random.fold_in(splits[3], 71), 0),
        "panel_embeds": draw_panel_embeds(jax.random.fold_in(splits[3], 71), 0),
        "trailing": bell_draw(splits[2], (ROWS, SLAB), 1.0, 6.0, ((0, 32), (1, 16)), jnp.float32),
    }


GAMMA = 0.45
RIDGE = 0.5

def squares(embeds):
    return jnp.einsum('ik,ik->i', embeds.astype(jnp.float32), embeds.astype(jnp.float32), preferred_element_type=jnp.float32)

def inner(left, right):
    return lax.dot_general(left.astype(jnp.float32), right.astype(jnp.float32), (((1,), (1,)), ((), ())), preferred_element_type=jnp.float32)

def reference(row_embeds, panel_embeds, trailing):
    norms_rows = squares(row_embeds)
    norms_panel = squares(panel_embeds)
    gram_rows = inner(row_embeds, panel_embeds)
    gram_diag = inner(panel_embeds, panel_embeds)
    kernel_diag = jnp.exp(-GAMMA * (norms_panel[:, None] + norms_panel[None, :] - 2.0 * gram_diag))
    kernel_diag = kernel_diag + RIDGE * jnp.eye(PANEL, dtype=jnp.float32)
    kernel_rows = jnp.exp(-GAMMA * (norms_rows[:, None] + norms_panel[None, :] - 2.0 * gram_rows))
    factor = jnp.linalg.cholesky(kernel_diag)
    panel = lax.linalg.triangular_solve(factor, kernel_rows, left_side=False, lower=True, transpose_a=True)
    top = panel[:SLAB]
    update = lax.dot_general(panel.astype(jnp.float32), top.astype(jnp.float32), (((1,), (1,)), ((), ())), precision=lax.Precision.HIGHEST, preferred_element_type=jnp.float32)
    return (panel, trailing - update)
```

```python
import functools
import jax
import jax.numpy as jnp
from jax import lax
from jax.experimental import pallas as pl
from jax.experimental.pallas import tpu as pltpu
from jax.sharding import PartitionSpec as P

MESH = pl.DeviceIdType.MESH

def gather_kernel(X, Z, Y, row_ref, pan_ref, xp, xr, xt, rdup, pdup, rsib, psib, rmine, pmine,
                  s_send, s_recv, p_send, p_recv, ps_send, ps_recv, r_send, r_recv, rs_send, rs_recv,
                  t1_send, t1_recv, t2_send, t2_recv, t3_send, t3_recv):
    R = row_ref.shape[0]
    H = R // 2
    NP = pan_ref.shape[0]
    NB = pdup.shape[0]
    BH = NP // NB // 2
    F = 128
    row = lax.axis_index("row")
    col = lax.axis_index("col")
    x, z = row // Z, row % Z
    y, k = col // 2, col % 2
    dev = lambda x, z, y, k: (x * Z + z, y * 2 + k)
    sib = dev(x, z, y, 1 - k)
    ypeer = lambda d: dev(x, z, lax.rem(y + d, Y), k)
    xpeer = lambda d: dev(lax.rem(x + d, X), z, y, k)
    zpeer = lambda d: dev(x, lax.rem(z + d, Z), y, k)
    cols = lambda yy: pl.ds(pl.multiple_of(yy * F, F), F)
    is_src = x == 0
    self_src = jnp.logical_and(x == 0, z == y)

    barrier = pltpu.get_barrier_semaphore()
    def signal(d):
        pl.semaphore_signal(barrier, inc=1, device_id=d, device_id_type=MESH)
    signal(sib)
    for d in range(1, Y):
        signal(ypeer(d))
    for d in range(1, X):
        signal(xpeer(d))
    for d in range(1, Z):
        signal(zpeer(d))
    for ys in range(Y):
        @pl.when(jnp.logical_not(jnp.logical_and(self_src, ys == y)))
        def _():
            signal(dev(0, y, ys, k))

    rv = row_ref[...]
    rdup[...] = jnp.concatenate([rv, rv], axis=1)
    pv = pan_ref[...]
    pdup[...] = jnp.concatenate([pv, pv], axis=1).reshape(pdup.shape)

    pl.semaphore_wait(barrier, 1 + (Y - 1) + (X - 1) + (Z - 1)
                      + jnp.where(is_src, X * Z, 0) - jnp.where(self_src, 1, 0))

    def remote(src, dst, ss, rs, to):
        return pltpu.make_async_remote_copy(src_ref=src, dst_ref=dst, send_sem=ss, recv_sem=rs,
                                            device_id=to, device_id_type=MESH)
    def drain(ref, sem):
        pltpu.make_async_copy(ref, ref, sem).wait()

    c1 = remote(pdup.at[:, 1 - k], psib, s_send.at[0], s_recv.at[0], sib)
    c1.start()
    c2 = remote(rdup.at[pl.ds(pl.multiple_of((1 - k) * H, H), H)], rsib, s_send.at[1], s_recv.at[1], sib)
    c2.start()
    c1.wait()
    lane = lax.broadcasted_iota(jnp.int32, (NB * BH, F), 1)
    keep = (lane < F // 2) == (k == 0)
    pm = jnp.where(keep, pdup[:, k].reshape(NB * BH, F).astype(jnp.float32),
                   psib[...].reshape(NB * BH, F).astype(jnp.float32)).astype(jnp.bfloat16)
    pmine[...] = pm.reshape(NB, BH, F)
    prow = lambda q, kk: pl.ds(pl.multiple_of(q * 2 * BH + kk * BH, BH), BH)
    for q in range(NB):
        for d in range(1, Y):
            remote(pmine.at[q], xp.at[prow(q, k), cols(y)], p_send, p_recv.at[q], ypeer(d)).start()
    for q in range(NB):
        xp[prow(q, k), cols(y)] = pmine[q]
    c2.wait()
    lane = lax.broadcasted_iota(jnp.int32, (H, F), 1)
    keep = (lane < F // 2) == (k == 0)
    rmine[...] = jnp.where(keep, rdup[pl.ds(pl.multiple_of(k * H, H), H)].astype(jnp.float32),
                           rsib[...].astype(jnp.float32)).astype(jnp.bfloat16)
    PC = H // (X * Z)
    @pl.when(is_src)
    def _():
        def body(i, c):
            to = dev(lax.rem(i, X), i // X, z, k)
            src = rmine.at[pl.ds(pl.multiple_of(i * PC, PC), PC)]
            dst = xt.at[pl.ds(pl.multiple_of(i * PC, PC), PC), cols(y)]
            me = jnp.logical_and(self_src, jnp.logical_and(lax.rem(i, X) == x, i // X == z))
            @pl.when(me)
            def _():
                pltpu.make_async_copy(src, dst, t1_recv).start()
            @pl.when(jnp.logical_not(me))
            def _():
                remote(src, dst, t1_send, t1_recv, to).start()
            return c
        lax.fori_loop(0, X * Z, body, 0)
    hrow = pl.ds(pl.multiple_of(k * H, H), H)
    for d in range(1, Y):
        remote(rmine, xr.at[hrow, cols(y)], r_send, r_recv.at[d - 1], ypeer(d)).start()
    xr[hrow, cols(y)] = rmine[...]
    rs = [remote(xr.at[hrow, cols(y)], xr.at[hrow, cols(y)], rs_send, rs_recv, sib)]
    rs[0].start()

    for q in range(NB):
        drain(xp.at[pl.ds(0, BH), pl.ds(0, (Y - 1) * F)], p_recv.at[q])
        remote(xp.at[prow(q, k)], xp.at[prow(q, k)], ps_send, ps_recv.at[q], sib).start()
    tp = pl.ds(pl.multiple_of((z * X + x) * PC, PC), PC)
    drain(xt.at[pl.ds(0, PC)], t1_recv)
    for d in range(1, X):
        remote(xt.at[tp], xt.at[tp], t2_send, t2_recv, xpeer(d)).start()
    drain(xt.at[pl.ds(0, (X - 1) * PC)], t2_recv)
    tz = pl.ds(pl.multiple_of(z * X * PC, X * PC), X * PC)
    for d in range(1, Z):
        remote(xt.at[tz], xt.at[tz], t3_send, t3_recv, zpeer(d)).start()
    for q in range(NB):
        drain(xp.at[pl.ds(0, BH)], ps_recv.at[q])
    for d in range(1, Y):
        drain(xr.at[pl.ds(0, H), pl.ds(0, F)], r_recv.at[d - 1])
        cc = cols(lax.rem(y + Y - d, Y))
        remote(xr.at[hrow, cc], xr.at[hrow, cc], rs_send, rs_recv, sib).start()
    drain(xt.at[pl.ds(0, (Z - 1) * X * PC)], t3_recv)
    drain(xr.at[pl.ds(0, H)], rs_recv)
    drain(xp.at[pl.ds(0, NB * BH), pl.ds(0, (Y - 1) * F)], p_send)
    drain(xp.at[pl.ds(0, NB * BH)], ps_send)
    drain(xr.at[pl.ds(0, H), pl.ds(0, (Y - 1) * F)], r_send)
    drain(xr.at[pl.ds(0, H)], rs_send)
    @pl.when(self_src)
    def _():
        drain(rmine.at[pl.ds(0, H - PC)], t1_send)
    @pl.when(jnp.logical_and(is_src, jnp.logical_not(self_src)))
    def _():
        drain(rmine, t1_send)
    drain(xt.at[pl.ds(0, (X - 1) * PC)], t2_send)
    drain(xt.at[pl.ds(0, (Z - 1) * X * PC)], t3_send)


def gather(X, Z, Y, row_embeds, panel_embeds, NB=4):
    R, NP = row_embeds.shape[0], panel_embeds.shape[0]
    H, BH, F = R // 2, NP // NB // 2, 128
    bf = jnp.bfloat16
    V = pltpu.VMEM
    D = pltpu.SemaphoreType.DMA
    vm = pl.BlockSpec(memory_space=pltpu.VMEM)
    return pl.pallas_call(
        functools.partial(gather_kernel, X, Z, Y),
        out_shape=[jax.ShapeDtypeStruct((NP, Y * F), bf), jax.ShapeDtypeStruct((R, Y * F), bf), jax.ShapeDtypeStruct((H, Y * F), bf)],
        in_specs=[vm, vm], out_specs=[vm, vm, vm],
        scratch_shapes=[V((R, F), bf), V((NB, 2, BH, F), bf), V((H, F), bf), V((NB, BH, F), bf), V((H, F), bf), V((NB, BH, F), bf),
                        D((2,)), D((2,)), D, D((NB,)), D, D((NB,)), D, D((Y - 1,)), D, D, D, D, D, D, D, D],
        compiler_params=pltpu.CompilerParams(collective_id=0, has_side_effects=True, vmem_limit_bytes=40 << 20),
    )(row_embeds, panel_embeds)


HI = lax.Precision.HIGHEST

def block8(rows, k, sub, lane):
    r_k = rows[k]
    inblk = (lane >= 8 * k) & (lane < 8 * k + 8)
    eye = (lane == 8 * k + sub)
    cols = [jnp.broadcast_to(r_k[:, 8 * k + l: 8 * k + l + 1], (8, 128)) for l in range(8)]
    start = jnp.where(inblk, jnp.where(eye, 1.0, 0.0), r_k)
    y = start
    z = start
    scale = jnp.ones((8, 128), jnp.float32)
    for p in range(8):
        piv = jnp.broadcast_to(cols[p][p:p + 1, :], (8, 128))
        r = 1.0 / piv
        t = cols[p] * r
        f = jnp.where(sub == p, 1.0 - r, t)
        for l in range(p + 1, 8):
            cols[l] = cols[l] - f * jnp.broadcast_to(cols[l][p:p + 1, :], (8, 128))
        y = y - f * jnp.broadcast_to(y[p:p + 1, :], (8, 128))
        scale = jnp.where(sub == p, lax.rsqrt(piv), scale)
        if p < 7:
            z = z - jnp.where(sub > p, t, 0.0) * jnp.broadcast_to(z[p:p + 1, :], (8, 128))
    rows[k] = z * scale
    yb = [jnp.broadcast_to(y[l:l + 1, :], (8, 128)) for l in range(8)]
    for m in range(k + 1, len(rows)):
        r_m = rows[m]
        prods = [jnp.broadcast_to(r_m[:, 8 * k + l: 8 * k + l + 1], (8, 128)) * yb[l] for l in range(8)]
        while len(prods) > 1:
            prods = [prods[i] + prods[i + 1] for i in range(0, len(prods), 2)]
        rows[m] = jnp.where(inblk, 0.0, r_m) - prods[0]
    return rows

def factor128(m_ref, at):
    sub = lax.broadcasted_iota(jnp.int32, (8, 128), 0)
    lane = lax.broadcasted_iota(jnp.int32, (8, 128), 1)
    rows = [m_ref[pl.ds(at + 8 * k, 8), pl.ds(at, 128)] for k in range(16)]
    for k in range(16):
        rows = block8(rows, k, sub, lane)
    for k in range(16):
        m_ref[pl.ds(at + 8 * k, 8), pl.ds(at, 128)] = jnp.where(lane <= sub + 8 * k, rows[k], 0.0)

def factor(m_ref, n=512):
    nb = n // 128
    for kb in range(nb):
        at = kb * 128
        factor128(m_ref, at)
        w = m_ref[at:at + 128, at:at + 128]
        if kb > 0:
            m_ref[at:at + 128, 0:at] = jnp.dot(w, m_ref[at:at + 128, 0:at], precision=HI, preferred_element_type=jnp.float32)
        if kb < nb - 1:
            u = jnp.dot(w, m_ref[at:at + 128, at + 128:n], precision=HI, preferred_element_type=jnp.float32)
            m_ref[at:at + 128, at + 128:n] = u
            left = m_ref[at:at + 128, 0:at + 128]
            upd = lax.dot_general(u, u, (((0,), (0,)), ((), ())), precision=HI, preferred_element_type=jnp.float32)
            m_ref[at + 128:n, at + 128:n] = m_ref[at + 128:n, at + 128:n] - upd
            low = lax.dot_general(u, left, (((0,), (0,)), ((), ())), precision=HI, preferred_element_type=jnp.float32)
            if kb > 0:
                m_ref[at + 128:n, 0:at] = m_ref[at + 128:n, 0:at] - low[:, :at]
            m_ref[at + 128:n, at:at + 128] = -low[:, at:]


GAMMA = 0.45
RIDGE = 0.5
NT = (((1,), (1,)), ((), ()))


def split(v):
    hi = v.astype(jnp.bfloat16)
    return hi, (v - hi.astype(jnp.float32)).astype(jnp.bfloat16)


def dot_nt(a, b):
    return lax.dot_general(a, b, NT, preferred_element_type=jnp.float32)


def compute_kernel(xp, xr, xt, tr_ref, panel_ref, up_ref, m_ref, whi, wlo, tb, tin, tout, nrow, sem_in, sem_out):
    NP = xp.shape[0]
    CH = 256
    R, S = xr.shape[0], xt.shape[0]
    NC = R // CH
    col = lax.axis_index("col")
    load = pltpu.make_async_copy(tr_ref, tin, sem_in)
    load.start()
    ri = lax.broadcasted_iota(jnp.int32, (NP, NP), 0)
    ci = lax.broadcasted_iota(jnp.int32, (NP, NP), 1)
    g = dot_nt(xp[...], xp[...])
    gd = jnp.where(ri == ci, g, 0.0)
    n_col = jnp.sum(gd, axis=1, keepdims=True)
    n_row = jnp.sum(gd, axis=0, keepdims=True)
    nrow[...] = jnp.broadcast_to(n_row, (8, NP))
    kd = jnp.exp(-GAMMA * (n_col + n_row - 2.0 * g))
    m_ref[...] = jnp.where(ri == ci, kd + RIDGE, kd)
    factor(m_ref, NP)
    w = jnp.where(ci <= ri, m_ref[...], 0.0)
    hi, lo = split(w)
    whi[...] = hi
    wlo[...] = lo

    def solve(xc):
        xf = xc.astype(jnp.float32)
        n = jnp.sum(xf * xf, axis=1, keepdims=True)
        kr = jnp.exp(-GAMMA * (n + nrow[0:1, :] - 2.0 * dot_nt(xc, xp[...])))
        khi, klo = split(kr)
        return dot_nt(khi, whi[...]) + (dot_nt(khi, wlo[...]) + dot_nt(klo, whi[...]))

    def top(i, c):
        at = pl.ds(pl.multiple_of(i * CH, CH), CH)
        tb[at] = solve(xt[at]).astype(jnp.bfloat16)
        return c
    lax.fori_loop(0, S // CH, top, 0)
    load.wait()
    tile = pl.ds(pl.multiple_of(col // 4 * 128, 128), 128)

    def rows(i, c):
        at = pl.ds(pl.multiple_of(i * CH, CH), CH)
        p = solve(xr[at])
        m_ref[pl.ds(0, CH)] = p
        own = pltpu.roll(m_ref[pl.ds(0, CH), tile], lax.rem(128 - lax.rem(col, 4) * 32, 128), 1)
        panel_ref[at] = own[:, 0:32]
        tout[at] = tin[at] - dot_nt(p.astype(jnp.bfloat16), tb[...])
        pltpu.make_async_copy(tout.at[at], up_ref.at[at], sem_out.at[i]).start()
        return c
    lax.fori_loop(0, NC, rows, 0)
    for i in range(NC):
        at = pl.ds(i * CH, CH)
        pltpu.make_async_copy(tout.at[at], up_ref.at[at], sem_out.at[i]).wait()


def compute(xp, xr, xt, trailing):
    NP, (R, S) = xp.shape[0], trailing.shape
    vm = pl.BlockSpec(memory_space=pltpu.VMEM)
    hbm = pl.BlockSpec(memory_space=pl.ANY)
    V = pltpu.VMEM
    f32, bf = jnp.float32, jnp.bfloat16
    return pl.pallas_call(
        compute_kernel,
        out_shape=[jax.ShapeDtypeStruct((R, 32), f32), jax.ShapeDtypeStruct((R, S), f32)],
        in_specs=[vm, vm, vm, hbm], out_specs=[vm, hbm],
        scratch_shapes=[V((NP, NP), f32), V((NP, NP), bf), V((NP, NP), bf), V((S, NP), bf), V((R, S), f32), V((R, S), f32),
                        V((8, NP), f32), pltpu.SemaphoreType.DMA, pltpu.SemaphoreType.DMA((R // 256,))],
        compiler_params=pltpu.CompilerParams(vmem_limit_bytes=48 << 20),
    )(xp, xr, xt, trailing)


def on_device(row_embeds, panel_embeds, trailing):
    xp, xr, xt = gather(4, 8, 8, row_embeds, panel_embeds)
    return compute(xp, xr, xt, trailing)


def solution(mesh):
    return jax.shard_map(
        on_device,
        mesh=mesh,
        in_specs=(P("row", "col"), P(None, "col"), P("row", "col")),
        out_specs=(P("row", "col"), P("row", "col")),
        check_vma=False,
    )
```

```python
import jax
import jax.numpy as jnp
from jax import lax
from jax.experimental import pallas as pl
from jax.experimental.pallas import tpu as pltpu
from jax.sharding import PartitionSpec as P

MESH = pl.DeviceIdType.MESH
X, Z, Y = 4, 8, 8
FEATS = 64
PIECE = FEATS // X
FIRST = 128
SEMS = ("p0", "p0s", "p1", "p1x", "p1s", "ra", "rb", "rs", "t1", "t2", "ta", "tb")


def rows_at(at, size):
    return pl.ds(pl.multiple_of(at, size), size)


class Gather:
    def __init__(self, row_ref, pan_ref, xp, xr, xt, send, recv):
        self.row_ref, self.pan_ref, self.xp, self.xr, self.xt = row_ref, pan_ref, xp, xr, xt
        self.send, self.recv = send, recv
        row, col = lax.axis_index("row"), lax.axis_index("col")
        self.x, self.z = row // Z, row % Z
        self.y, self.k = col // 2, col % 2
        self.top = xt.shape[1]

    def dev(self, x=None, z=None, y=None, k=None):
        x, z, y, k = (a if b is None else b for a, b in zip((self.x, self.z, self.y, self.k), (x, z, y, k)))
        return (x * Z + z, y * 2 + k)

    def ynext(self, d):
        return lax.rem(self.y + d + Y, Y)

    def znext(self, d):
        return lax.rem(self.z + d + Z, Z)

    def copy(self, name, src, dst, to):
        i = SEMS.index(name)
        pltpu.make_async_remote_copy(src_ref=src, dst_ref=dst, send_sem=self.send.at[i], recv_sem=self.recv.at[i],
                                     device_id=to, device_id_type=MESH).start()

    def arrived(self, name, ref):
        pltpu.make_async_copy(ref, ref, self.recv.at[SEMS.index(name)]).wait()

    def sent(self, name, ref):
        pltpu.make_async_copy(ref, ref, self.send.at[SEMS.index(name)]).wait()

    def is_self_source(self):
        return jnp.logical_and(self.x == 0, self.z == self.y)

    def barrier(self):
        sem = pltpu.get_barrier_semaphore()

        def signal(to):
            pl.semaphore_signal(sem, inc=1, device_id=to, device_id_type=MESH)

        signal(self.dev(k=1 - self.k))
        for d in range(1, Y):
            signal(self.dev(y=self.ynext(d)))
        for d in range(1, X):
            signal(self.dev(x=lax.rem(self.x + d, X)))
        for d in (-2, -1, 1, 2):
            signal(self.dev(z=self.znext(d)))
        mine = self.is_self_source()
        for ks in range(2):
            @pl.when(jnp.logical_not(jnp.logical_and(mine, self.k == ks)))
            def _():
                signal(self.dev(x=0, z=self.y, y=self.z, k=ks))
        pl.semaphore_wait(sem, 1 + (Y - 1) + (X - 1) + 4 + jnp.where(self.x == 0, 2 * X, 0) - jnp.where(mine, 1, 0))

    def panel_start(self):
        x, y, k = self.x, self.y, self.k
        for d in range(1, Y):
            self.copy("p0", self.pan_ref.at[:, pl.ds(0, FIRST)], self.xp.at[y, k, :, pl.ds(0, FIRST)], self.dev(y=self.ynext(d)))
        piece, rest = rows_at(x * PIECE, PIECE), pl.ds(FIRST, self.pan_ref.shape[1] - FIRST)
        for d in range(1, Y):
            self.copy("p1", self.pan_ref.at[piece, rest], self.xp.at[y, k, piece, rest], self.dev(y=self.ynext(d)))
        self.xp[y, k, :, pl.ds(0, FIRST)] = self.pan_ref[:, pl.ds(0, FIRST)]
        self.xp[y, k, piece, rest] = self.pan_ref[piece, rest]

    def panel_first_to_sibling(self):
        self.arrived("p0", self.xp.at[pl.ds(0, Y - 1), 0, :, pl.ds(0, FIRST)])
        part = self.xp.at[:, self.k, :, pl.ds(0, FIRST)]
        self.copy("p0s", part, part, self.dev(k=1 - self.k))

    def panel_first_done(self):
        self.arrived("p0s", self.xp.at[:, 0, :, pl.ds(0, FIRST)])

    def panel_rest_along_x(self):
        rest = pl.ds(FIRST, self.pan_ref.shape[1] - FIRST)
        self.arrived("p1", self.xp.at[pl.ds(0, Y - 1), 0, pl.ds(0, PIECE), rest])
        part = self.xp.at[:, self.k, rows_at(self.x * PIECE, PIECE), rest]
        for d in range(1, X):
            self.copy("p1x", part, part, self.dev(x=lax.rem(self.x + d, X)))

    def panel_rest_to_sibling(self):
        rest = pl.ds(FIRST, self.pan_ref.shape[1] - FIRST)
        self.arrived("p1x", self.xp.at[:, 0, pl.ds(0, (X - 1) * PIECE), rest])
        part = self.xp.at[:, self.k, :, rest]
        self.copy("p1s", part, part, self.dev(k=1 - self.k))

    def panel_rest_done(self):
        rest = pl.ds(FIRST, self.pan_ref.shape[1] - FIRST)
        self.arrived("p1s", self.xp.at[:, 0, :, rest])

    def row_chunk(self, d, half=None):
        at = self.ynext(d) * 2 * FEATS + self.k * FEATS
        if half is None:
            return self.xr.at[rows_at(at, FEATS)]
        return self.xr.at[rows_at(at + half * (FEATS // 2), FEATS // 2)]

    def rows_start(self):
        own = self.row_chunk(0)
        for d in (1, -1, 2, -2):
            self.copy("ra", self.row_ref, own, self.dev(y=self.ynext(d)))
        self.copy("rs", self.row_ref, own, self.dev(k=1 - self.k))
        self.xr[rows_at(self.y * 2 * FEATS + self.k * FEATS, FEATS)] = self.row_ref[...]

    def rows_forward(self):
        self.arrived("ra", self.xr.at[pl.ds(0, 4 * FEATS)])
        for d, to, half in ((2, -1, None), (-2, 1, None), (-2, 2, 0), (2, -2, 1)):
            self.copy("rb", self.row_chunk(d, half), self.row_chunk(d, half), self.dev(y=self.ynext(to)))
        for d in (1, -1, 2, -2):
            self.copy("rs", self.row_chunk(d), self.row_chunk(d), self.dev(k=1 - self.k))

    def rows_last_to_sibling(self):
        self.arrived("rb", self.xr.at[pl.ds(0, 3 * FEATS)])
        for d in (3, -3, 4):
            self.copy("rs", self.row_chunk(d), self.row_chunk(d), self.dev(k=1 - self.k))

    def rows_done(self):
        self.arrived("rs", self.xr.at[pl.ds(0, Y * FEATS)])

    def top_start(self):
        for kc in range(2):
            for xd in range(X):
                src = self.row_ref.at[pl.ds(xd * PIECE, PIECE), pl.ds(kc * self.top, self.top)]
                dst = self.xt.at[rows_at(self.y * 2 * FEATS + self.k * FEATS + xd * PIECE, PIECE)]
                me = jnp.logical_and(self.is_self_source(), jnp.logical_and(self.k == kc, xd == 0))

                @pl.when(me)
                def _():
                    pltpu.make_async_copy(src, dst, self.recv.at[SEMS.index("t1")]).start()

                @pl.when(jnp.logical_and(self.x == 0, jnp.logical_not(me)))
                def _():
                    self.copy("t1", src, dst, self.dev(x=xd, z=self.y, y=self.z, k=kc))

    def top_along_x(self):
        self.arrived("t1", self.xt.at[pl.ds(0, 2 * PIECE)])
        for kk in range(2):
            part = self.xt.at[rows_at((self.z * 2 + kk) * FEATS + self.x * PIECE, PIECE)]
            for d in range(1, X):
                self.copy("t2", part, part, self.dev(x=lax.rem(self.x + d, X)))

    def top_chunk(self, d, half=None):
        at = self.znext(d) * 2 * FEATS
        if half is None:
            return self.xt.at[rows_at(at, 2 * FEATS)]
        return self.xt.at[rows_at(at + half * FEATS, FEATS)]

    def top_along_z(self):
        self.arrived("t2", self.xt.at[pl.ds(0, 2 * (X - 1) * PIECE)])
        for d in (1, -1, 2, -2):
            self.copy("ta", self.top_chunk(0), self.top_chunk(0), self.dev(z=self.znext(d)))

    def top_forward(self):
        self.arrived("ta", self.xt.at[pl.ds(0, 4 * 2 * FEATS)])
        for d, to, half in ((2, -1, None), (-2, 1, None), (-2, 2, 0), (2, -2, 1)):
            self.copy("tb", self.top_chunk(d, half), self.top_chunk(d, half), self.dev(z=self.znext(to)))

    def top_done(self):
        self.arrived("tb", self.xt.at[pl.ds(0, 3 * 2 * FEATS)])

    def all_sent(self):
        rest = pl.ds(FIRST, self.pan_ref.shape[1] - FIRST)
        self.sent("p0", self.xp.at[pl.ds(0, Y - 1), 0, :, pl.ds(0, FIRST)])
        self.sent("p0s", self.xp.at[:, 0, :, pl.ds(0, FIRST)])
        self.sent("p1", self.xp.at[pl.ds(0, Y - 1), 0, pl.ds(0, PIECE), rest])
        self.sent("p1x", self.xp.at[:, 0, pl.ds(0, (X - 1) * PIECE), rest])
        self.sent("p1s", self.xp.at[:, 0, :, rest])
        self.sent("ra", self.xr.at[pl.ds(0, 4 * FEATS)])
        self.sent("rb", self.xr.at[pl.ds(0, 3 * FEATS)])
        self.sent("rs", self.xr.at[pl.ds(0, Y * FEATS)])
        mine = self.is_self_source()

        @pl.when(jnp.logical_and(self.x == 0, jnp.logical_not(mine)))
        def _():
            self.sent("t1", self.xt.at[pl.ds(0, 2 * X * PIECE)])

        @pl.when(mine)
        def _():
            self.sent("t1", self.xt.at[pl.ds(0, (2 * X - 1) * PIECE)])
        self.sent("t2", self.xt.at[pl.ds(0, 2 * (X - 1) * PIECE)])
        self.sent("ta", self.xt.at[pl.ds(0, 4 * 2 * FEATS)])
        self.sent("tb", self.xt.at[pl.ds(0, 3 * 2 * FEATS)])


B = 16
HI = lax.Precision.HIGHEST


def spread_row(v, p):
    return jnp.broadcast_to(v[..., p:p + 1, :], v.shape)


def spread_col(v, l):
    return jnp.broadcast_to(v[..., l:l + 1], v.shape)


def subtract_products(r, at, yb):
    parts = [spread_col(r, at + l) * yb[l] for l in range(B)]
    while len(parts) > 1:
        parts = [parts[i] + parts[i + 1] for i in range(0, len(parts), 2)]
    return parts[0]


def eliminate(now, rest, k, sub, lane):
    at = B * k
    inblk = (lane >= at) & (lane < at + B)
    cols = jnp.stack([spread_col(now, at + l) for l in range(B)])
    y = jnp.where(inblk, jnp.where(lane == at + sub, 1.0, 0.0), now)
    z = y
    scale = jnp.ones(now.shape, jnp.float32)
    for p in range(0, B, 2):
        q = p + 1
        a, b = cols[0], cols[1]
        app, aqp, bqq = spread_row(a, p), spread_row(a, q), spread_row(b, q)
        det = app * bqq - aqp * aqp
        r = 1.0 / det
        ae = a - jnp.where(sub == p, 1.0, 0.0)
        be = b - jnp.where(sub == q, 1.0, 0.0)
        f0 = (ae * bqq - be * aqp) * r
        f1 = (be * app - ae * aqp) * r
        if q < B - 1:
            cols = cols[2:]
            cols = cols - (f0[None] * spread_row(cols, p) + f1[None] * spread_row(cols, q))
        y = y - (f0 * spread_row(y, p) + f1 * spread_row(y, q))
        s = lax.rsqrt(app)
        inv = s * s
        scale = jnp.where(sub == p, s, jnp.where(sub == q, lax.rsqrt(det * inv), scale))
        g0 = jnp.where(sub > q, f0, jnp.where(sub == q, aqp * inv, 0.0))
        g1 = jnp.where(sub > q, f1, 0.0)
        z = z - (g0 * spread_row(z, p) + g1 * spread_row(z, q))
    done = z * scale
    if rest is None:
        return done, None, None
    yb = [spread_row(y, l) for l in range(B)]
    first = jnp.where(inblk, 0.0, rest[0]) - subtract_products(rest[0], at, yb)
    if rest.shape[0] == 1:
        return done, first, None
    tail = rest[1:]
    new = jnp.where(inblk[None], 0.0, tail)
    for l in range(B):
        new = new - spread_col(tail, at + l) * yb[l][None]
    return done, first, new


def factor128(m_ref, at, hook=None):
    sub = lax.broadcasted_iota(jnp.int32, (B, 128), 0)
    lane = lax.broadcasted_iota(jnp.int32, (B, 128), 1)
    n = 128 // B
    block = m_ref[pl.ds(at, 128), pl.ds(at, 128)].reshape(n, B, 128)
    now, rest = block[0], block[1:]
    for k in range(n):
        done, now, rest = eliminate(now, rest, k, sub, lane)
        m_ref[pl.ds(at + B * k, B), pl.ds(at, 128)] = jnp.where(lane <= sub + B * k, done, 0.0)
        if hook is not None and k == n // 2 - 1:
            hook()

GAMMA = 0.45
RIDGE = 0.5
CHUNK = 256
TN = (((0,), (0,)), ((), ()))


def mul(a, b):
    return jnp.dot(a, b, preferred_element_type=jnp.float32)


def mul_exact(a, b):
    return jnp.dot(a, b, precision=HI, preferred_element_type=jnp.float32)


def mul_tn(a, b, precision=None):
    return lax.dot_general(a, b, TN, precision=precision, preferred_element_type=jnp.float32)


def split(v):
    hi = v.astype(jnp.bfloat16)
    return hi, (v - hi.astype(jnp.float32)).astype(jnp.bfloat16)


def diag_kernel(gram):
    n = gram.shape[0]
    same = lax.broadcasted_iota(jnp.int32, (n, n), 0) == lax.broadcasted_iota(jnp.int32, (n, n), 1)
    on = jnp.where(same, gram, 0.0)
    col, row = jnp.sum(on, axis=1, keepdims=True), jnp.sum(on, axis=0, keepdims=True)
    kd = jnp.exp(-GAMMA * (col + row - 2.0 * gram))
    return jnp.where(same, kd + RIDGE, kd), col


def spread_block(m_ref, at):
    n = m_ref.shape[0]
    end = at + 128
    w = m_ref[at:end, at:end]
    if at > 0:
        m_ref[at:end, 0:at] = mul_exact(w, m_ref[at:end, 0:at])
    if end < n:
        u = mul_exact(w, m_ref[at:end, end:n])
        m_ref[end:n, end:n] = m_ref[end:n, end:n] - mul_tn(u, u, HI)
        low = mul_tn(u, m_ref[at:end, 0:end], HI)
        if at > 0:
            m_ref[end:n, 0:at] = m_ref[end:n, 0:at] - low[:, :at]
        m_ref[end:n, at:end] = -low[:, at:]


def step_kernel(row_ref, pan_ref, tr_ref, panel_ref, up_ref, xp, xr, xt, xn, m, whi, wlo, tt, pt, tin, tout, norm,
                send, recv, sem_in, sem_out):
    g = Gather(row_ref, pan_ref, xp, xr, xt, send, recv)
    load = pltpu.make_async_copy(tr_ref, tin, sem_in)
    load.start()
    g.barrier()
    g.panel_start()
    g.top_start()
    g.rows_start()
    g.panel_first_to_sibling()
    g.panel_rest_along_x()
    g.top_along_x()
    g.panel_first_done()
    np_, feats = xn.shape
    first = xp[:, :, :, pl.ds(0, FIRST)].reshape(feats, FIRST)
    m[pl.ds(0, FIRST), pl.ds(0, FIRST)] = diag_kernel(mul_tn(first, first))[0]

    def after_first():
        g.panel_rest_to_sibling()
        g.top_along_z()
    factor128(m, 0, after_first)
    g.panel_rest_done()
    whole = xp[...].reshape(feats, np_)
    xn[...] = whole.T
    kd, col = diag_kernel(mul(xn[...], whole))
    norm[...] = jnp.broadcast_to(col, norm.shape)
    m[pl.ds(0, FIRST), pl.ds(FIRST, np_ - FIRST)] = kd[:FIRST, FIRST:]
    m[pl.ds(FIRST, np_ - FIRST), pl.ds(FIRST, np_ - FIRST)] = kd[FIRST:, FIRST:]
    spread_block(m, 0)
    factor128(m, 128)
    spread_block(m, 128)
    factor128(m, 256, g.rows_forward)
    spread_block(m, 256)
    g.top_forward()
    factor128(m, 384)
    spread_block(m, 384)
    ri = lax.broadcasted_iota(jnp.int32, (np_, np_), 0)
    ci = lax.broadcasted_iota(jnp.int32, (np_, np_), 1)
    hi, lo = split(jnp.where(ci <= ri, m[...], 0.0))
    whi[...] = hi
    wlo[...] = lo
    g.rows_last_to_sibling()

    def solve(xc):
        xf = xc.astype(jnp.float32)
        n = jnp.sum(xf * xf, axis=0, keepdims=True)
        k = jnp.exp(-GAMMA * (norm[:, 0:1] + n - 2.0 * mul(xn[...], xc)))
        khi, klo = split(k)
        return mul(whi[...], khi) + (mul(whi[...], klo) + mul(wlo[...], khi))

    g.top_done()
    for i in range(xt.shape[1] // CHUNK):
        at = pl.ds(i * CHUNK, CHUNK)
        tt[:, at] = solve(xt[:, at]).astype(jnp.bfloat16)
    g.rows_done()
    load.wait()
    own = rows_at(lax.axis_index("col") * panel_ref.shape[0], panel_ref.shape[0])
    chunks = tin.shape[0] // CHUNK
    for i in range(chunks):
        at = pl.ds(i * CHUNK, CHUNK)
        p = solve(xr[:, at])
        pt[...] = p
        panel_ref[:, at] = pt[own, :]
        tout[at, :] = tin[at, :] - mul_tn(p.astype(jnp.bfloat16), tt[...])
        pltpu.make_async_copy(tout.at[at], up_ref.at[at], sem_out.at[i]).start()
    for i in range(chunks):
        at = pl.ds(i * CHUNK, CHUNK)
        pltpu.make_async_copy(tout.at[at], up_ref.at[at], sem_out.at[i]).wait()
    g.all_sent()


def on_device(row_embeds, panel_embeds, trailing):
    rows, slab = trailing.shape
    np_ = panel_embeds.shape[0]
    feats = Y * 2 * FEATS
    vm = pl.BlockSpec(memory_space=pltpu.VMEM)
    hbm = pl.BlockSpec(memory_space=pl.ANY)
    V, D = pltpu.VMEM, pltpu.SemaphoreType.DMA
    f32, bf = jnp.float32, jnp.bfloat16
    panel, updated = pl.pallas_call(
        step_kernel,
        out_shape=[jax.ShapeDtypeStruct((np_ // (2 * Y), rows), f32), jax.ShapeDtypeStruct((rows, slab), f32)],
        in_specs=[vm, vm, hbm],
        out_specs=[vm, hbm],
        scratch_shapes=[
            V((Y, 2, FEATS, np_), bf), V((feats, rows), bf), V((feats, slab), bf), V((np_, feats), bf),
            V((np_, np_), f32), V((np_, np_), bf), V((np_, np_), bf), V((np_, slab), bf), V((np_, CHUNK), f32),
            V((rows, slab), f32), V((rows, slab), f32), V((np_, 128), f32),
            D((len(SEMS),)), D((len(SEMS),)), D, D((rows // CHUNK,)),
        ],
        compiler_params=pltpu.CompilerParams(collective_id=0, has_side_effects=True, vmem_limit_bytes=48 << 20),
    )(row_embeds.T, panel_embeds.T, trailing)
    return panel.T, updated


def solution(mesh):
    return jax.shard_map(
        on_device,
        mesh=mesh,
        in_specs=(P("row", "col"), P(None, "col"), P("row", "col")),
        out_specs=(P("row", "col"), P("row", "col")),
        check_vma=False,
    )
```

```python
import jax
import jax.numpy as jnp
from jax import lax
from jax.experimental import pallas as pl
from jax.experimental.pallas import tpu as pltpu
from jax.sharding import PartitionSpec as P

MESH = pl.DeviceIdType.MESH
X, Z, Y = 4, 8, 8
FEATS = 64
PIECE = FEATS // X
FIRST = 128
SEMS = ("p0", "p0s", "p1", "p1x", "p1s", "ra", "rb", "rs", "t0", "t1", "ux", "ua", "ub", "vz", "vx",
        "rl", "tl")


def rows_at(at, size):
    return pl.ds(pl.multiple_of(at, size), size)


class Gather:
    def __init__(self, row_ref, pan_ref, xp, xr, xt, spread, send, recv):
        self.row_ref, self.pan_ref, self.xp, self.xr, self.xt, self.spread = row_ref, pan_ref, xp, xr, xt, spread
        self.send, self.recv = send, recv
        row, col = lax.axis_index("row"), lax.axis_index("col")
        self.x, self.z = row // Z, row % Z
        self.y, self.k = col // 2, col % 2
        self.top = xt.shape[-1]

    def dev(self, x=None, z=None, y=None, k=None):
        x, z, y, k = (a if b is None else b for a, b in zip((self.x, self.z, self.y, self.k), (x, z, y, k)))
        return (x * Z + z, y * 2 + k)

    def ynext(self, d):
        return lax.rem(self.y + d + Y, Y)

    def znext(self, d):
        return lax.rem(self.z + d + Z, Z)

    def copy(self, name, src, dst, to):
        i = SEMS.index(name)
        pltpu.make_async_remote_copy(src_ref=src, dst_ref=dst, send_sem=self.send.at[i], recv_sem=self.recv.at[i],
                                     device_id=to, device_id_type=MESH).start()

    def arrived(self, name, ref):
        pltpu.make_async_copy(ref, ref, self.recv.at[SEMS.index(name)]).wait()

    def sent(self, name, ref):
        pltpu.make_async_copy(ref, ref, self.send.at[SEMS.index(name)]).wait()

    def local(self, name, src, dst, when):
        @pl.when(when)
        def _():
            pltpu.make_async_copy(src, dst, self.recv.at[SEMS.index(name)]).start()

    def barrier(self):
        sem = pltpu.get_barrier_semaphore()

        def signal(to):
            pl.semaphore_signal(sem, inc=1, device_id=to, device_id_type=MESH)

        signal(self.dev(k=1 - self.k))
        for d in range(1, Y):
            signal(self.dev(y=self.ynext(d)))
        for d in range(1, X):
            signal(self.dev(x=lax.rem(self.x + d, X)))
        for d in range(1, Z):
            signal(self.dev(z=self.znext(d)))
        same = self.z == self.y
        for ks in range(2):
            @pl.when(jnp.logical_not(jnp.logical_and(same, self.k == ks)))
            def _():
                signal(self.dev(z=self.y, y=self.z, k=ks))
        pl.semaphore_wait(sem, 1 + (Y - 1) + (X - 1) + (Z - 1) + 2 - jnp.where(same, 1, 0))

    def panel_start(self):
        x, y, k = self.x, self.y, self.k
        for d in range(1, Y):
            self.copy("p0", self.pan_ref.at[:, pl.ds(0, FIRST)], self.xp.at[y, k, :, pl.ds(0, FIRST)], self.dev(y=self.ynext(d)))
        piece, rest = rows_at(x * PIECE, PIECE), pl.ds(FIRST, self.pan_ref.shape[1] - FIRST)
        for d in range(1, Y):
            self.copy("p1", self.pan_ref.at[piece, rest], self.xp.at[y, k, piece, rest], self.dev(y=self.ynext(d)))
        pltpu.make_async_copy(self.pan_ref.at[:, pl.ds(0, FIRST)], self.xp.at[y, k, :, pl.ds(0, FIRST)], self.recv.at[SEMS.index("p0")]).start()
        pltpu.make_async_copy(self.pan_ref.at[piece, rest], self.xp.at[y, k, piece, rest], self.recv.at[SEMS.index("p1")]).start()

    def panel_first_to_sibling(self):
        self.arrived("p0", self.xp.at[:, 0, :, pl.ds(0, FIRST)])
        part = self.xp.at[:, self.k, :, pl.ds(0, FIRST)]
        self.copy("p0s", part, part, self.dev(k=1 - self.k))

    def panel_first_done(self):
        self.arrived("p0s", self.xp.at[:, 0, :, pl.ds(0, FIRST)])

    def panel_rest_along_x(self):
        rest = pl.ds(FIRST, self.pan_ref.shape[1] - FIRST)
        self.arrived("p1", self.xp.at[:, 0, pl.ds(0, PIECE), rest])
        part = self.xp.at[:, self.k, rows_at(self.x * PIECE, PIECE), rest]
        for d in range(1, X):
            self.copy("p1x", part, part, self.dev(x=lax.rem(self.x + d, X)))

    def panel_rest_to_sibling(self):
        rest = pl.ds(FIRST, self.pan_ref.shape[1] - FIRST)
        self.arrived("p1x", self.xp.at[:, 0, pl.ds(0, (X - 1) * PIECE), rest])
        part = self.xp.at[:, self.k, :, rest]
        self.copy("p1s", part, part, self.dev(k=1 - self.k))

    def panel_rest_done(self):
        rest = pl.ds(FIRST, self.pan_ref.shape[1] - FIRST)
        self.arrived("p1s", self.xp.at[:, 0, :, rest])

    def row_chunk(self, d, half=None):
        at = self.ynext(d) * 2 * FEATS + self.k * FEATS
        if half is None:
            return self.xr.at[rows_at(at, FEATS)]
        return self.xr.at[rows_at(at + half * (FEATS // 2), FEATS // 2)]

    def rows_start(self):
        own = self.row_chunk(0)
        for d in (1, -1, 2, -2):
            self.copy("ra", self.row_ref, own, self.dev(y=self.ynext(d)))
        self.copy("rs", self.row_ref, own, self.dev(k=1 - self.k))
        pltpu.make_async_copy(self.row_ref, own, self.recv.at[SEMS.index("rl")]).start()

    def rows_forward(self):
        self.arrived("ra", self.xr.at[pl.ds(0, 4 * FEATS)])
        for d, to, half in ((2, -1, None), (-2, 1, None), (-2, 2, 0), (2, -2, 1)):
            self.copy("rb", self.row_chunk(d, half), self.row_chunk(d, half), self.dev(y=self.ynext(to)))
        for d in (1, -1, 2, -2):
            self.copy("rs", self.row_chunk(d), self.row_chunk(d), self.dev(k=1 - self.k))

    def rows_last_to_sibling(self):
        self.arrived("rb", self.xr.at[pl.ds(0, 3 * FEATS)])
        for d in (3, -3, 4):
            self.copy("rs", self.row_chunk(d), self.row_chunk(d), self.dev(k=1 - self.k))

    def rows_done(self):
        self.arrived("rl", self.row_chunk(0))
        self.arrived("rs", self.xr.at[pl.ds(0, Y * FEATS)])

    def own_piece(self, half):
        return pl.ds(half * self.top, self.top)

    def top_start(self):
        self.local("tl", self.row_ref.at[pl.ds(0, PIECE)], self.spread, self.x == 0)

        @pl.when(self.x == 0)
        def _():
            for xd in range(1, X):
                self.copy("t0", self.row_ref.at[pl.ds(xd * PIECE, PIECE)], self.spread, self.dev(x=xd))

    def top_to_plane(self):
        @pl.when(self.x == 0)
        def _():
            self.arrived("tl", self.spread)

        @pl.when(self.x != 0)
        def _():
            self.arrived("t0", self.spread)
        same = self.z == self.y
        for kc in range(2):
            src, dst = self.spread.at[:, self.own_piece(kc)], self.xt.at[self.y, self.k, self.x]
            me = jnp.logical_and(same, self.k == kc)
            self.local("t1", src, dst, me)

            @pl.when(jnp.logical_not(me))
            def _():
                self.copy("t1", src, dst, self.dev(z=self.y, y=self.z, k=kc))

    def top_spread(self):
        self.arrived("t1", self.xt.at[0, :, 0])
        part = self.xt.at[self.z, 0, self.x]
        for d in range(1, X):
            self.copy("ux", part, part, self.dev(x=lax.rem(self.x + d, X)))
        part = self.xt.at[self.z, 1, self.x]
        for d in range(1, Z):
            self.copy("vz", part, part, self.dev(z=self.znext(d)))

    def top_chunk(self, d, half=None):
        if half is None:
            return self.xt.at[self.znext(d), 0]
        return self.xt.at[self.znext(d), 0, pl.ds(half * (X // 2), X // 2)]

    def top_along_z(self):
        self.arrived("ux", self.xt.at[0, 0, pl.ds(0, X - 1)])
        for d in (1, -1, 2, -2):
            self.copy("ua", self.top_chunk(0), self.top_chunk(0), self.dev(z=self.znext(d)))

    def top_along_x(self):
        self.arrived("vz", self.xt.at[pl.ds(0, Z - 1), 0, 0])
        part = self.xt.at[:, 1, self.x]
        for d in range(1, X):
            self.copy("vx", part, part, self.dev(x=lax.rem(self.x + d, X)))

    def top_forward(self):
        self.arrived("ua", self.xt.at[pl.ds(0, 4), 0])
        for d, to, half in ((2, -1, None), (-2, 1, None), (-2, 2, 0), (2, -2, 1)):
            self.copy("ub", self.top_chunk(d, half), self.top_chunk(d, half), self.dev(z=self.znext(to)))

    def top_done(self):
        self.arrived("ub", self.xt.at[pl.ds(0, 3), 0])
        self.arrived("vx", self.xt.at[:, 0, pl.ds(0, X - 1)])

    def all_sent(self):
        rest = pl.ds(FIRST, self.pan_ref.shape[1] - FIRST)
        self.sent("p0", self.xp.at[pl.ds(0, Y - 1), 0, :, pl.ds(0, FIRST)])
        self.sent("p0s", self.xp.at[:, 0, :, pl.ds(0, FIRST)])
        self.sent("p1", self.xp.at[pl.ds(0, Y - 1), 0, pl.ds(0, PIECE), rest])
        self.sent("p1x", self.xp.at[:, 0, pl.ds(0, (X - 1) * PIECE), rest])
        self.sent("p1s", self.xp.at[:, 0, :, rest])
        self.sent("ra", self.xr.at[pl.ds(0, 4 * FEATS)])
        self.sent("rb", self.xr.at[pl.ds(0, 3 * FEATS)])
        self.sent("rs", self.xr.at[pl.ds(0, Y * FEATS)])

        @pl.when(self.x == 0)
        def _():
            self.sent("t0", self.row_ref.at[pl.ds(0, (X - 1) * PIECE)])

        @pl.when(self.z == self.y)
        def _():
            self.sent("t1", self.xt.at[0, 0, 0])

        @pl.when(self.z != self.y)
        def _():
            self.sent("t1", self.xt.at[0, :, 0])
        self.sent("ux", self.xt.at[0, 0, pl.ds(0, X - 1)])
        self.sent("ua", self.xt.at[pl.ds(0, 4), 0])
        self.sent("ub", self.xt.at[pl.ds(0, 3), 0])
        self.sent("vz", self.xt.at[pl.ds(0, Z - 1), 0, 0])
        self.sent("vx", self.xt.at[:, 0, pl.ds(0, X - 1)])


B = 16
HI = lax.Precision.HIGHEST


def spread_row(v, p):
    return jnp.broadcast_to(v[..., p:p + 1, :], v.shape)


def spread_col(v, l):
    return jnp.broadcast_to(v[..., l:l + 1], v.shape)


def subtract_products(r, at, yb):
    parts = [spread_col(r, at + l) * yb[l] for l in range(B)]
    while len(parts) > 1:
        parts = [parts[i] + parts[i + 1] for i in range(0, len(parts), 2)]
    return parts[0]


def eliminate(now, rest, k, sub, lane):
    at = B * k
    inblk = (lane >= at) & (lane < at + B)
    cols = jnp.stack([spread_col(now, at + l) for l in range(B)])
    y = jnp.where(inblk, jnp.where(lane == at + sub, 1.0, 0.0), now)
    z = y
    scale = jnp.ones(now.shape, jnp.float32)
    for p in range(0, B, 2):
        q = p + 1
        a, b = cols[0], cols[1]
        app, aqp, bqq = spread_row(a, p), spread_row(a, q), spread_row(b, q)
        det = app * bqq - aqp * aqp
        r = 1.0 / det
        ae = a - jnp.where(sub == p, 1.0, 0.0)
        be = b - jnp.where(sub == q, 1.0, 0.0)
        f0 = (ae * bqq - be * aqp) * r
        f1 = (be * app - ae * aqp) * r
        if q < B - 1:
            cols = cols[2:]
            cols = cols - (f0[None] * spread_row(cols, p) + f1[None] * spread_row(cols, q))
        y = y - (f0 * spread_row(y, p) + f1 * spread_row(y, q))
        s = lax.rsqrt(app)
        inv = s * s
        scale = jnp.where(sub == p, s, jnp.where(sub == q, lax.rsqrt(det * inv), scale))
        g0 = jnp.where(sub > q, f0, jnp.where(sub == q, aqp * inv, 0.0))
        g1 = jnp.where(sub > q, f1, 0.0)
        z = z - (g0 * spread_row(z, p) + g1 * spread_row(z, q))
    done = z * scale
    if rest is None:
        return done, None, None
    yb = [spread_row(y, l) for l in range(B)]
    first = jnp.where(inblk, 0.0, rest[0]) - subtract_products(rest[0], at, yb)
    if rest.shape[0] == 1:
        return done, first, None
    tail = rest[1:]
    new = jnp.where(inblk[None], 0.0, tail)
    for l in range(B):
        new = new - spread_col(tail, at + l) * yb[l][None]
    return done, first, new


def factor128(m_ref, at, hook=None):
    sub = lax.broadcasted_iota(jnp.int32, (B, 128), 0)
    lane = lax.broadcasted_iota(jnp.int32, (B, 128), 1)
    n = 128 // B
    block = m_ref[pl.ds(at, 128), pl.ds(at, 128)].reshape(n, B, 128)
    now, rest = block[0], block[1:]
    for k in range(n):
        done, now, rest = eliminate(now, rest, k, sub, lane)
        m_ref[pl.ds(at + B * k, B), pl.ds(at, 128)] = jnp.where(lane <= sub + B * k, done, 0.0)
        if hook is not None and k == n // 2 - 1:
            hook()

GAMMA = 0.45
RIDGE = 0.5
CHUNK = 512
TN = (((0,), (0,)), ((), ()))


def mul(a, b):
    return jnp.dot(a, b, preferred_element_type=jnp.float32)


def mul_exact(a, b):
    return jnp.dot(a, b, precision=HI, preferred_element_type=jnp.float32)


def mul_tn(a, b, precision=None):
    return lax.dot_general(a, b, TN, precision=precision, preferred_element_type=jnp.float32)


def split(v):
    hi = v.astype(jnp.bfloat16)
    return hi, (v - hi.astype(jnp.float32)).astype(jnp.bfloat16)


def diag_kernel(gram):
    n = gram.shape[0]
    same = lax.broadcasted_iota(jnp.int32, (n, n), 0) == lax.broadcasted_iota(jnp.int32, (n, n), 1)
    on = jnp.where(same, gram, 0.0)
    col, row = jnp.sum(on, axis=1, keepdims=True), jnp.sum(on, axis=0, keepdims=True)
    kd = jnp.exp(-GAMMA * (col + row - 2.0 * gram))
    return jnp.where(same, kd + RIDGE, kd), col


def spread_block(m_ref, at):
    n = m_ref.shape[0]
    end = at + 128
    w = m_ref[at:end, at:end]
    if at > 0:
        m_ref[at:end, 0:at] = mul_exact(w, m_ref[at:end, 0:at])
    if end < n:
        u = mul_exact(w, m_ref[at:end, end:n])
        m_ref[end:n, end:n] = m_ref[end:n, end:n] - mul_tn(u, u, HI)
        low = mul_tn(u, m_ref[at:end, 0:end], HI)
        if at > 0:
            m_ref[end:n, 0:at] = m_ref[end:n, 0:at] - low[:, :at]
        m_ref[end:n, at:end] = -low[:, at:]


def step_kernel(row_ref, pan_ref, tr_ref, panel_ref, up_ref, xp, xr, xt, xn, m, whi, wlo, tt, pt, tin, tout, norm,
                spread, send, recv, sem_in, sem_out):
    g = Gather(row_ref, pan_ref, xp, xr, xt, spread, send, recv)
    load = pltpu.make_async_copy(tr_ref, tin, sem_in)
    load.start()
    g.barrier()
    g.panel_start()
    g.top_start()
    g.top_to_plane()
    g.rows_start()
    g.panel_first_to_sibling()
    g.panel_rest_along_x()
    g.panel_first_done()
    np_, feats = xn.shape
    first = xp[:, :, :, pl.ds(0, FIRST)].reshape(feats, FIRST)
    m[pl.ds(0, FIRST), pl.ds(0, FIRST)] = diag_kernel(mul_tn(first, first))[0]

    def after_first():
        g.panel_rest_to_sibling()
        g.top_spread()
    factor128(m, 0, after_first)
    g.panel_rest_done()
    whole = xp[...].reshape(feats, np_)
    xn[...] = whole.T
    kd, col = diag_kernel(mul(xn[...], whole))
    norm[...] = jnp.broadcast_to(col, norm.shape)
    m[pl.ds(0, FIRST), pl.ds(FIRST, np_ - FIRST)] = kd[:FIRST, FIRST:]
    m[pl.ds(FIRST, np_ - FIRST), pl.ds(FIRST, np_ - FIRST)] = kd[FIRST:, FIRST:]
    spread_block(m, 0)
    g.top_along_z()
    factor128(m, 128, g.top_along_x)
    spread_block(m, 128)
    factor128(m, 256, g.rows_forward)
    spread_block(m, 256)
    g.top_forward()
    factor128(m, 384)
    spread_block(m, 384)
    ri = lax.broadcasted_iota(jnp.int32, (np_, np_), 0)
    ci = lax.broadcasted_iota(jnp.int32, (np_, np_), 1)
    hi, lo = split(jnp.where(ci <= ri, m[...], 0.0))
    whi[...] = hi
    wlo[...] = lo
    g.rows_last_to_sibling()

    def solve(xc):
        xf = xc.astype(jnp.float32)
        n = jnp.sum(xf * xf, axis=0, keepdims=True)
        k = jnp.exp(-GAMMA * (norm[:, 0:1] + n - 2.0 * mul(xn[...], xc)))
        khi, klo = split(k)
        half = k.shape[0] // 2
        top = pl.ds(0, half), pl.ds(0, half)
        low = pl.ds(half, half)
        first = mul(whi[top], khi[:half]) + (mul(whi[top], klo[:half]) + mul(wlo[top], khi[:half]))
        second = mul(whi[low, :], khi) + (mul(whi[low, :], klo) + mul(wlo[low, :], khi))
        return first, second

    g.top_done()
    for i in range(xt.shape[-1] // CHUNK):
        at = pl.ds(i * CHUNK, CHUNK)
        for j, p in enumerate(solve(xt[:, :, :, :, at].reshape(feats, CHUNK))):
            tt[pl.ds(j * (np_ // 2), np_ // 2), at] = p.astype(jnp.bfloat16)
    g.rows_done()
    load.wait()
    own = rows_at(lax.axis_index("col") * panel_ref.shape[0], panel_ref.shape[0])
    chunks = tin.shape[0] // CHUNK
    for i in range(chunks):
        at = pl.ds(i * CHUNK, CHUNK)
        out = tin[at, :]
        for j, p in enumerate(solve(xr[:, at])):
            half = pl.ds(j * (np_ // 2), np_ // 2)
            pt[half, at] = p
            out = out - mul_tn(p.astype(jnp.bfloat16), tt[half, :])
        tout[at, :] = out
        pltpu.make_async_copy(tout.at[at], up_ref.at[at], sem_out.at[i]).start()
    panel_ref[...] = pt[own, :]
    for i in range(chunks):
        at = pl.ds(i * CHUNK, CHUNK)
        pltpu.make_async_copy(tout.at[at], up_ref.at[at], sem_out.at[i]).wait()
    g.all_sent()


def on_device(row_embeds, panel_embeds, trailing):
    rows, slab = trailing.shape
    np_ = panel_embeds.shape[0]
    feats = Y * 2 * FEATS
    vm = pl.BlockSpec(memory_space=pltpu.VMEM)
    hbm = pl.BlockSpec(memory_space=pl.ANY)
    V, D = pltpu.VMEM, pltpu.SemaphoreType.DMA
    f32, bf = jnp.float32, jnp.bfloat16
    panel, updated = pl.pallas_call(
        step_kernel,
        out_shape=[jax.ShapeDtypeStruct((np_ // (2 * Y), rows), f32), jax.ShapeDtypeStruct((rows, slab), f32)],
        in_specs=[hbm, hbm, hbm],
        out_specs=[vm, hbm],
        scratch_shapes=[
            V((Y, 2, FEATS, np_), bf), V((feats, rows), bf), V((Y, 2, X, PIECE, slab), bf), V((np_, feats), bf),
            V((np_, np_), f32), V((np_, np_), bf), V((np_, np_), bf), V((np_, slab), bf), V((np_, rows), f32),
            V((rows, slab), f32), V((rows, slab), f32), V((np_, 128), f32), V((PIECE, rows), bf),
            D((len(SEMS),)), D((len(SEMS),)), D, D((rows // CHUNK,)),
        ],
        compiler_params=pltpu.CompilerParams(collective_id=0, has_side_effects=True, vmem_limit_bytes=63 << 20),
    )(row_embeds.T, panel_embeds.T, trailing)
    return panel.T, updated


def solution(mesh):
    return jax.shard_map(
        on_device,
        mesh=mesh,
        in_specs=(P("row", "col"), P(None, "col"), P("row", "col")),
        out_specs=(P("row", "col"), P("row", "col")),
        check_vma=False,
    )
```

```python
import jax
import jax.numpy as jnp
from jax import lax
from jax.experimental import pallas as pl
from jax.experimental.pallas import tpu as pltpu
from jax.sharding import PartitionSpec as P

MESH = pl.DeviceIdType.MESH
X, Z, Y = 4, 8, 8
FEATS = 64
PIECE = FEATS // X
FIRST = 128
SEMS = ("p0", "p0s", "p1", "p1x", "p1s", "ra", "rb", "rs", "t0", "t1", "ux", "ua", "ub", "vz", "vx",
        "rl", "tl")


def rows_at(at, size):
    return pl.ds(pl.multiple_of(at, size), size)


class Gather:
    def __init__(self, row_ref, pan_ref, xp, xr, xt, spread, send, recv):
        self.row_ref, self.pan_ref, self.xp, self.xr, self.xt, self.spread = row_ref, pan_ref, xp, xr, xt, spread
        self.send, self.recv = send, recv
        row, col = lax.axis_index("row"), lax.axis_index("col")
        self.x, self.z = row // Z, row % Z
        self.y, self.k = col // 2, col % 2
        self.top = xt.shape[-1]

    def dev(self, x=None, z=None, y=None, k=None):
        x, z, y, k = (a if b is None else b for a, b in zip((self.x, self.z, self.y, self.k), (x, z, y, k)))
        return (x * Z + z, y * 2 + k)

    def ynext(self, d):
        return lax.rem(self.y + d + Y, Y)

    def znext(self, d):
        return lax.rem(self.z + d + Z, Z)

    def copy(self, name, src, dst, to):
        i = SEMS.index(name)
        pltpu.make_async_remote_copy(src_ref=src, dst_ref=dst, send_sem=self.send.at[i], recv_sem=self.recv.at[i],
                                     device_id=to, device_id_type=MESH).start()

    def arrived(self, name, ref):
        pltpu.make_async_copy(ref, ref, self.recv.at[SEMS.index(name)]).wait()

    def sent(self, name, ref):
        pltpu.make_async_copy(ref, ref, self.send.at[SEMS.index(name)]).wait()

    def local(self, name, src, dst, when):
        @pl.when(when)
        def _():
            pltpu.make_async_copy(src, dst, self.recv.at[SEMS.index(name)]).start()

    def barrier(self):
        sem = pltpu.get_barrier_semaphore()

        def signal(to):
            pl.semaphore_signal(sem, inc=1, device_id=to, device_id_type=MESH)

        signal(self.dev(k=1 - self.k))
        for d in range(1, Y):
            signal(self.dev(y=self.ynext(d)))
        for d in range(1, X):
            signal(self.dev(x=lax.rem(self.x + d, X)))
        for d in range(1, Z):
            signal(self.dev(z=self.znext(d)))
        same = self.z == self.y
        for ks in range(2):
            @pl.when(jnp.logical_not(jnp.logical_and(same, self.k == ks)))
            def _():
                signal(self.dev(z=self.y, y=self.z, k=ks))
        pl.semaphore_wait(sem, 1 + (Y - 1) + (X - 1) + (Z - 1) + 2 - jnp.where(same, 1, 0))

    def panel_start(self):
        x, y, k = self.x, self.y, self.k
        for d in range(1, Y):
            self.copy("p0", self.pan_ref.at[:, pl.ds(0, FIRST)], self.xp.at[y, k, :, pl.ds(0, FIRST)], self.dev(y=self.ynext(d)))
        piece, rest = rows_at(x * PIECE, PIECE), pl.ds(FIRST, self.pan_ref.shape[1] - FIRST)
        for d in range(1, Y):
            self.copy("p1", self.pan_ref.at[piece, rest], self.xp.at[y, k, piece, rest], self.dev(y=self.ynext(d)))
        pltpu.make_async_copy(self.pan_ref.at[:, pl.ds(0, FIRST)], self.xp.at[y, k, :, pl.ds(0, FIRST)], self.recv.at[SEMS.index("p0")]).start()
        pltpu.make_async_copy(self.pan_ref.at[piece, rest], self.xp.at[y, k, piece, rest], self.recv.at[SEMS.index("p1")]).start()

    def panel_first_to_sibling(self):
        self.arrived("p0", self.xp.at[:, 0, :, pl.ds(0, FIRST)])
        part = self.xp.at[:, self.k, :, pl.ds(0, FIRST)]
        self.copy("p0s", part, part, self.dev(k=1 - self.k))

    def panel_first_done(self):
        self.arrived("p0s", self.xp.at[:, 0, :, pl.ds(0, FIRST)])

    def panel_rest_along_x(self):
        rest = pl.ds(FIRST, self.pan_ref.shape[1] - FIRST)
        self.arrived("p1", self.xp.at[:, 0, pl.ds(0, PIECE), rest])
        part = self.xp.at[:, self.k, rows_at(self.x * PIECE, PIECE), rest]
        for d in range(1, X):
            self.copy("p1x", part, part, self.dev(x=lax.rem(self.x + d, X)))

    def panel_rest_to_sibling(self):
        rest = pl.ds(FIRST, self.pan_ref.shape[1] - FIRST)
        self.arrived("p1x", self.xp.at[:, 0, pl.ds(0, (X - 1) * PIECE), rest])
        part = self.xp.at[:, self.k, :, rest]
        self.copy("p1s", part, part, self.dev(k=1 - self.k))

    def panel_rest_done(self):
        rest = pl.ds(FIRST, self.pan_ref.shape[1] - FIRST)
        self.arrived("p1s", self.xp.at[:, 0, :, rest])

    def row_chunk(self, d, half=None):
        at = self.ynext(d) * 2 * FEATS + self.k * FEATS
        if half is None:
            return self.xr.at[rows_at(at, FEATS)]
        return self.xr.at[rows_at(at + half * (FEATS // 2), FEATS // 2)]

    def rows_start(self):
        own = self.row_chunk(0)
        for d in (1, -1, 2, -2):
            self.copy("ra", self.row_ref, own, self.dev(y=self.ynext(d)))
        self.copy("rs", self.row_ref, own, self.dev(k=1 - self.k))
        pltpu.make_async_copy(self.row_ref, own, self.recv.at[SEMS.index("rl")]).start()

    def rows_forward(self):
        self.arrived("ra", self.xr.at[pl.ds(0, 4 * FEATS)])
        for d, to, half in ((2, -1, None), (-2, 1, None), (-2, 2, 0), (2, -2, 1)):
            self.copy("rb", self.row_chunk(d, half), self.row_chunk(d, half), self.dev(y=self.ynext(to)))
        for d in (1, -1, 2, -2):
            self.copy("rs", self.row_chunk(d), self.row_chunk(d), self.dev(k=1 - self.k))

    def rows_last_to_sibling(self):
        self.arrived("rb", self.xr.at[pl.ds(0, 3 * FEATS)])
        for d in (3, -3, 4):
            self.copy("rs", self.row_chunk(d), self.row_chunk(d), self.dev(k=1 - self.k))

    def rows_done(self):
        self.arrived("rl", self.row_chunk(0))
        self.arrived("rs", self.xr.at[pl.ds(0, Y * FEATS)])

    def own_piece(self, half):
        return pl.ds(half * self.top, self.top)

    def top_start(self):
        self.local("tl", self.row_ref.at[pl.ds(0, PIECE)], self.spread, self.x == 0)

        @pl.when(self.x == 0)
        def _():
            for xd in range(1, X):
                self.copy("t0", self.row_ref.at[pl.ds(xd * PIECE, PIECE)], self.spread, self.dev(x=xd))

    def top_to_plane(self):
        @pl.when(self.x == 0)
        def _():
            self.arrived("tl", self.spread)

        @pl.when(self.x != 0)
        def _():
            self.arrived("t0", self.spread)
        same = self.z == self.y
        for kc in range(2):
            src, dst = self.spread.at[:, self.own_piece(kc)], self.xt.at[self.y, self.k, self.x]
            me = jnp.logical_and(same, self.k == kc)
            self.local("t1", src, dst, me)

            @pl.when(jnp.logical_not(me))
            def _():
                self.copy("t1", src, dst, self.dev(z=self.y, y=self.z, k=kc))

    def top_spread(self):
        self.arrived("t1", self.xt.at[0, :, 0])
        part = self.xt.at[self.z, 0, self.x]
        for d in range(1, X):
            self.copy("ux", part, part, self.dev(x=lax.rem(self.x + d, X)))
        part = self.xt.at[self.z, 1, self.x]
        for d in range(1, Z):
            self.copy("vz", part, part, self.dev(z=self.znext(d)))

    def top_chunk(self, d, half=None):
        if half is None:
            return self.xt.at[self.znext(d), 0]
        return self.xt.at[self.znext(d), 0, pl.ds(half * (X // 2), X // 2)]

    def top_along_z(self):
        self.arrived("ux", self.xt.at[0, 0, pl.ds(0, X - 1)])
        for d in (1, -1, 2, -2):
            self.copy("ua", self.top_chunk(0), self.top_chunk(0), self.dev(z=self.znext(d)))

    def top_along_x(self):
        self.arrived("vz", self.xt.at[pl.ds(0, Z - 1), 0, 0])
        part = self.xt.at[:, 1, self.x]
        for d in range(1, X):
            self.copy("vx", part, part, self.dev(x=lax.rem(self.x + d, X)))

    def top_forward(self):
        self.arrived("ua", self.xt.at[pl.ds(0, 4), 0])
        for d, to, half in ((2, -1, None), (-2, 1, None), (-2, 2, 0), (2, -2, 1)):
            self.copy("ub", self.top_chunk(d, half), self.top_chunk(d, half), self.dev(z=self.znext(to)))

    def top_done(self):
        self.arrived("ub", self.xt.at[pl.ds(0, 3), 0])
        self.arrived("vx", self.xt.at[:, 0, pl.ds(0, X - 1)])

    def all_sent(self):
        rest = pl.ds(FIRST, self.pan_ref.shape[1] - FIRST)
        self.sent("p0", self.xp.at[pl.ds(0, Y - 1), 0, :, pl.ds(0, FIRST)])
        self.sent("p0s", self.xp.at[:, 0, :, pl.ds(0, FIRST)])
        self.sent("p1", self.xp.at[pl.ds(0, Y - 1), 0, pl.ds(0, PIECE), rest])
        self.sent("p1x", self.xp.at[:, 0, pl.ds(0, (X - 1) * PIECE), rest])
        self.sent("p1s", self.xp.at[:, 0, :, rest])
        self.sent("ra", self.xr.at[pl.ds(0, 4 * FEATS)])
        self.sent("rb", self.xr.at[pl.ds(0, 3 * FEATS)])
        self.sent("rs", self.xr.at[pl.ds(0, Y * FEATS)])

        @pl.when(self.x == 0)
        def _():
            self.sent("t0", self.row_ref.at[pl.ds(0, (X - 1) * PIECE)])

        @pl.when(self.z == self.y)
        def _():
            self.sent("t1", self.xt.at[0, 0, 0])

        @pl.when(self.z != self.y)
        def _():
            self.sent("t1", self.xt.at[0, :, 0])
        self.sent("ux", self.xt.at[0, 0, pl.ds(0, X - 1)])
        self.sent("ua", self.xt.at[pl.ds(0, 4), 0])
        self.sent("ub", self.xt.at[pl.ds(0, 3), 0])
        self.sent("vz", self.xt.at[pl.ds(0, Z - 1), 0, 0])
        self.sent("vx", self.xt.at[:, 0, pl.ds(0, X - 1)])


B = 16
HI = lax.Precision.HIGHEST


def spread_row(v, p):
    return jnp.broadcast_to(v[..., p:p + 1, :], v.shape)


def spread_col(v, l):
    return jnp.broadcast_to(v[..., l:l + 1], v.shape)


def subtract_products(r, at, yb):
    parts = [spread_col(r, at + l) * yb[l] for l in range(B)]
    while len(parts) > 1:
        parts = [parts[i] + parts[i + 1] for i in range(0, len(parts), 2)]
    return parts[0]


def eliminate(now, rest, k, sub, lane):
    at = B * k
    inblk = (lane >= at) & (lane < at + B)
    cols = jnp.stack([spread_col(now, at + l) for l in range(B)])
    y = jnp.where(inblk, jnp.where(lane == at + sub, 1.0, 0.0), now)
    z = y
    scale = jnp.ones(now.shape, jnp.float32)
    for p in range(0, B, 2):
        q = p + 1
        a, b = cols[0], cols[1]
        app, aqp, bqq = spread_row(a, p), spread_row(a, q), spread_row(b, q)
        det = app * bqq - aqp * aqp
        r = 1.0 / det
        ae = a - jnp.where(sub == p, 1.0, 0.0)
        be = b - jnp.where(sub == q, 1.0, 0.0)
        f0 = (ae * bqq - be * aqp) * r
        f1 = (be * app - ae * aqp) * r
        if q < B - 1:
            cols = cols[2:]
            cols = cols - (f0[None] * spread_row(cols, p) + f1[None] * spread_row(cols, q))
        y = y - (f0 * spread_row(y, p) + f1 * spread_row(y, q))
        s = lax.rsqrt(app)
        inv = s * s
        scale = jnp.where(sub == p, s, jnp.where(sub == q, lax.rsqrt(det * inv), scale))
        g0 = jnp.where(sub > q, f0, jnp.where(sub == q, aqp * inv, 0.0))
        g1 = jnp.where(sub > q, f1, 0.0)
        z = z - (g0 * spread_row(z, p) + g1 * spread_row(z, q))
    done = z * scale
    if rest is None:
        return done, None, None
    yb = [spread_row(y, l) for l in range(B)]
    first = jnp.where(inblk, 0.0, rest[0]) - subtract_products(rest[0], at, yb)
    if rest.shape[0] == 1:
        return done, first, None
    tail = rest[1:]
    new = jnp.where(inblk[None], 0.0, tail)
    for l in range(B):
        new = new - spread_col(tail, at + l) * yb[l][None]
    return done, first, new


def factor128(m_ref, at, hook=None):
    sub = lax.broadcasted_iota(jnp.int32, (B, 128), 0)
    lane = lax.broadcasted_iota(jnp.int32, (B, 128), 1)
    n = 128 // B
    block = m_ref[pl.ds(at, 128), pl.ds(at, 128)].reshape(n, B, 128)
    now, rest = block[0], block[1:]
    for k in range(n):
        done, now, rest = eliminate(now, rest, k, sub, lane)
        m_ref[pl.ds(at + B * k, B), pl.ds(at, 128)] = jnp.where(lane <= sub + B * k, done, 0.0)
        if hook is not None and k == n // 2 - 1:
            hook()

GAMMA = 0.45
RIDGE = 0.5
CHUNK = 512
TN = (((0,), (0,)), ((), ()))


def mul(a, b):
    return jnp.dot(a, b, preferred_element_type=jnp.float32)


def mul_exact(a, b):
    return jnp.dot(a, b, precision=HI, preferred_element_type=jnp.float32)


def mul_tn(a, b, precision=None):
    return lax.dot_general(a, b, TN, precision=precision, preferred_element_type=jnp.float32)


def split(v):
    hi = v.astype(jnp.bfloat16)
    return hi, (v - hi.astype(jnp.float32)).astype(jnp.bfloat16)


def diag_kernel(gram):
    n = gram.shape[0]
    same = lax.broadcasted_iota(jnp.int32, (n, n), 0) == lax.broadcasted_iota(jnp.int32, (n, n), 1)
    on = jnp.where(same, gram, 0.0)
    col, row = jnp.sum(on, axis=1, keepdims=True), jnp.sum(on, axis=0, keepdims=True)
    kd = jnp.exp(-GAMMA * (col + row - 2.0 * gram))
    return jnp.where(same, kd + RIDGE, kd), col


def spread_block(m_ref, at):
    n = m_ref.shape[0]
    end = at + 128
    w = m_ref[at:end, at:end]
    if at > 0:
        m_ref[at:end, 0:at] = mul_exact(w, m_ref[at:end, 0:at])
    if end < n:
        u = mul_exact(w, m_ref[at:end, end:n])
        m_ref[end:n, end:n] = m_ref[end:n, end:n] - mul_tn(u, u, HI)
        low = mul_tn(u, m_ref[at:end, 0:end], HI)
        if at > 0:
            m_ref[end:n, 0:at] = m_ref[end:n, 0:at] - low[:, :at]
        m_ref[end:n, at:end] = -low[:, at:]


def step_kernel(row_ref, pan_ref, panel_ref, up_ref, xp, xr, xt, xn, m, whi, wlo, tt, pt, tout, norm,
                spread, send, recv, sem_out):
    g = Gather(row_ref, pan_ref, xp, xr, xt, spread, send, recv)
    g.barrier()
    g.panel_start()
    g.top_start()
    g.top_to_plane()
    g.rows_start()
    g.panel_first_to_sibling()
    g.panel_rest_along_x()
    g.panel_first_done()
    np_, feats = xn.shape
    first = xp[:, :, :, pl.ds(0, FIRST)].reshape(feats, FIRST)
    m[pl.ds(0, FIRST), pl.ds(0, FIRST)] = diag_kernel(mul_tn(first, first))[0]

    def after_first():
        g.panel_rest_to_sibling()
        g.top_spread()
    factor128(m, 0, after_first)
    g.top_along_z()
    g.panel_rest_done()
    whole = xp[...].reshape(feats, np_)
    xn[...] = whole.T
    kd, col = diag_kernel(mul(xn[...], whole))
    norm[...] = jnp.broadcast_to(col, norm.shape)
    m[pl.ds(0, FIRST), pl.ds(FIRST, np_ - FIRST)] = kd[:FIRST, FIRST:]
    m[pl.ds(FIRST, np_ - FIRST), pl.ds(FIRST, np_ - FIRST)] = kd[FIRST:, FIRST:]
    spread_block(m, 0)
    factor128(m, 128, g.top_along_x)
    g.rows_forward()
    spread_block(m, 128)
    factor128(m, 256, g.top_forward)
    spread_block(m, 256)
    factor128(m, 384)
    spread_block(m, 384)
    ri = lax.broadcasted_iota(jnp.int32, (np_, np_), 0)
    ci = lax.broadcasted_iota(jnp.int32, (np_, np_), 1)
    hi, lo = split(jnp.where(ci <= ri, m[...], 0.0))
    whi[...] = hi
    wlo[...] = lo
    g.rows_last_to_sibling()

    def solve(xc):
        xf = xc.astype(jnp.float32)
        n = jnp.sum(xf * xf, axis=0, keepdims=True)
        k = jnp.exp(-GAMMA * (norm[:, 0:1] + n - 2.0 * mul(xn[...], xc)))
        khi, klo = split(k)
        half = k.shape[0] // 2
        top = pl.ds(0, half), pl.ds(0, half)
        low = pl.ds(half, half)
        first = mul(whi[top], khi[:half]) + (mul(whi[top], klo[:half]) + mul(wlo[top], khi[:half]))
        second = mul(whi[low, :], khi) + (mul(whi[low, :], klo) + mul(wlo[low, :], khi))
        return first, second

    g.top_done()
    for i in range(xt.shape[-1] // CHUNK):
        at = pl.ds(i * CHUNK, CHUNK)
        for j, p in enumerate(solve(xt[:, :, :, :, at].reshape(feats, CHUNK))):
            tt[pl.ds(j * (np_ // 2), np_ // 2), at] = p.astype(jnp.bfloat16)
    g.rows_done()
    own = rows_at(lax.axis_index("col") * panel_ref.shape[0], panel_ref.shape[0])
    chunks = tout.shape[0] // CHUNK
    for i in range(chunks):
        at = pl.ds(i * CHUNK, CHUNK)
        out = None
        for j, p in enumerate(solve(xr[:, at])):
            half = pl.ds(j * (np_ // 2), np_ // 2)
            pt[half, at] = p
            part = mul_tn(p.astype(jnp.bfloat16), tt[half, :])
            out = part if out is None else out + part
        tout[at, :] = out
        pltpu.make_async_copy(tout.at[at], up_ref.at[at], sem_out.at[i]).start()
    panel_ref[...] = pt[own, :]
    for i in range(chunks):
        at = pl.ds(i * CHUNK, CHUNK)
        pltpu.make_async_copy(tout.at[at], up_ref.at[at], sem_out.at[i]).wait()
    g.all_sent()


def on_device(row_embeds, panel_embeds, trailing):
    rows, slab = trailing.shape
    np_ = panel_embeds.shape[0]
    feats = Y * 2 * FEATS
    vm = pl.BlockSpec(memory_space=pltpu.VMEM)
    hbm = pl.BlockSpec(memory_space=pl.ANY)
    V, D = pltpu.VMEM, pltpu.SemaphoreType.DMA
    f32, bf = jnp.float32, jnp.bfloat16
    panel, update = pl.pallas_call(
        step_kernel,
        out_shape=[jax.ShapeDtypeStruct((np_ // (2 * Y), rows), f32), jax.ShapeDtypeStruct((rows, slab), f32)],
        in_specs=[hbm, hbm],
        out_specs=[vm, hbm],
        scratch_shapes=[
            V((Y, 2, FEATS, np_), bf), V((feats, rows), bf), V((Y, 2, X, PIECE, slab), bf), V((np_, feats), bf),
            V((np_, np_), f32), V((np_, np_), bf), V((np_, np_), bf), V((np_, slab), bf), V((np_, rows), f32),
            V((rows, slab), f32), V((np_, 128), f32), V((PIECE, rows), bf),
            D((len(SEMS),)), D((len(SEMS),)), D((rows // CHUNK,)),
        ],
        compiler_params=pltpu.CompilerParams(collective_id=0, has_side_effects=True, vmem_limit_bytes=40 << 20),
    )(row_embeds.T, panel_embeds.T)
    return panel.T, trailing - update


def solution(mesh):
    return jax.shard_map(
        on_device,
        mesh=mesh,
        in_specs=(P("row", "col"), P(None, "col"), P("row", "col")),
        out_specs=(P("row", "col"), P("row", "col")),
        check_vma=False,
    )
```
